1024 devices in a mesh: dp: 32 (over x, z_lo, core), expert: 32 (over y, z_hi).
Axes of the slice: x: 8, y: 8, z: 8 (z_hi: 4, z_lo: 2; z = z_hi * 2 + z_lo), core: 2. Of those that a mesh axis runs over, the one named last changes fastest.
Arguments:
- tokens: bfloat16 [1024, 256, 768], P(('dp', 'expert')), may hold values from -16 to 16
- cotangent: bfloat16 [1024, 256, 768], P(('dp', 'expert')), may hold values from -6 to 6
- router: bfloat16 [768, 32], replicated, may hold values from -1 to 1
- in_weights: bfloat16 [32, 768, 2560], P('expert'), may hold values from -0.21875 to 0.21875
- out_weights: bfloat16 [32, 2560, 768], P('expert'), may hold values from -0.125 to 0.125
Outputs:
- token_grad: bfloat16 [1024, 256, 768], P(('dp', 'expert'))
- router_grad: float32 [768, 32], replicated
- in_weight_grad: bfloat16 [2560, 32, 768], P('dp', 'expert')
- out_weight_grad: bfloat16 [2560, 32, 768], P('dp', 'expert')
The draws below stay inside these ranges and needn't reach their ends.
All inputs are finite; a program needn't handle non-finite values.
Results may differ from the reference program's by a relative error of at most 0.014.
Values may be sent and summed in bfloat16 or wider, within the bound.
A program may use at most 64 MiB of HBM per device.

```python
import math
import jax
import jax.numpy as jnp
from jax import lax

D = 768
FF = 2560
PATCHES = 256
EXPERTS = 32
IMAGES = 1024
N_DP = 32


def sign_table(key):
    flips = jax.random.bernoulli(key, 0.5, (D, EXPERTS))
    return jnp.where(flips, 1.0, -1.0).astype(jnp.float32) / math.sqrt(D)


def draw_router(key, part):
    table = sign_table(key)
    return table.astype(jnp.bfloat16)


def draw_tokens(key, part):
    key = jax.random.fold_in(key, 5)
    keys = jax.random.split(key, 1)
    values = jax.random.truncated_normal(keys[0], -6.0, 6.0, (IMAGES, PATCHES, D))
    return values.astype(jnp.bfloat16)


def levels(rng, extent, cuts, smallest, top_value):
    loudness = 1.0
    for axis_at, shards_of in cuts:
        steps = jax.random.uniform(jax.random.fold_in(jax.random.fold_in(rng, 6), axis_at), (shards_of,), jnp.float32, smallest / len(cuts), top_value / len(cuts))
        loudness = loudness * jnp.repeat(jnp.exp(steps), extent[axis_at] // shards_of).reshape((-1,) + (1,) * (len(extent) - 1 - axis_at))
    return loudness


def gaussian(stream_key, shape, spread, most, cuts=(), held_as=jnp.bfloat16):
    drawn = spread * jax.random.normal(stream_key, shape, jnp.float32)
    if cuts:
        drawn = drawn * levels(stream_key, shape, cuts, -0.22, 0.18)
    return jnp.clip(drawn, -most, most).astype(held_as)


def setup_inputs(seed: int = 0) -> dict:
    seeds = jax.random.split(jax.random.key(seed), 6)
    tokens = draw_tokens(jax.random.fold_in(seeds[5], 71), 0)
    cotangent = gaussian(seeds[1], (IMAGES, PATCHES, D), 1.0, 6.0, ((0, 1024),))
    router = draw_router(jax.random.fold_in(seeds[5], 71), 0)
    in_weights = gaussian(seeds[3], (EXPERTS, D, FF), D ** -0.5, 0.21875, ((0, 32),))
    out_weights = gaussian(seeds[4], (EXPERTS, FF, D), FF ** -0.5, 0.125, ((0, 32),))
    return {"tokens": tokens, "cotangent": cotangent, "router": router, "in_weights": in_weights, "out_weights": out_weights}


half_root = 0.7071067811865476
inv_root_two_pi = 0.3989422804014327


def lowered(values):
    return lax.optimization_barrier(values.astype(jnp.bfloat16)).astype(jnp.float32)


def gelu_parts(pre_act):
    normal_cdf = 0.5 * (1.0 + jax.scipy.special.erf(pre_act * half_root))
    normal_pdf = jnp.exp(-0.5 * pre_act * pre_act) * inv_root_two_pi
    return normal_cdf, normal_pdf


def probabilities(images, router):
    logits = jnp.einsum('bpd,ds->bsp', images.astype(jnp.float32), router.astype(jnp.float32))
    dispatch = jax.nn.softmax(logits, axis=2)
    combine = jax.nn.softmax(logits, axis=1)
    return dispatch, combine


def reference(tokens, cotangent, router, in_weights, out_weights):
    group = IMAGES // N_DP
    tok_blocks = tokens.reshape(N_DP, group, PATCHES, D)
    cot_blocks = cotangent.reshape(N_DP, group, PATCHES, D)

    def slot_pass(items):
        images, grads = items
        dispatch, combine = probabilities(images, router)
        slot_inputs = jnp.einsum('bsp,bpd->bsd', lowered(dispatch), images.astype(jnp.float32)).astype(jnp.bfloat16)
        slot_cotan = jnp.einsum('bsp,bpd->bsd', lowered(combine), grads.astype(jnp.float32)).astype(jnp.bfloat16)
        return slot_inputs, slot_cotan

    slot_inputs, slot_cotan = lax.map(slot_pass, (tok_blocks, cot_blocks))
    inputs_by_expert = jnp.swapaxes(slot_inputs.reshape(IMAGES, EXPERTS, D), 0, 1)
    cotan_by_expert = jnp.swapaxes(slot_cotan.reshape(IMAGES, EXPERTS, D), 0, 1)

    def expert_pass(items):
        rows_in, rows_cotan, first_weight, second_weight = items
        pre_act = jnp.dot(rows_in, first_weight, preferred_element_type=jnp.float32)
        normal_cdf, normal_pdf = gelu_parts(pre_act)
        hidden = (pre_act * normal_cdf).astype(jnp.bfloat16)
        outputs = jnp.dot(hidden, second_weight, preferred_element_type=jnp.float32).astype(jnp.bfloat16)
        hidden_grad = jnp.dot(rows_cotan, second_weight.T, preferred_element_type=jnp.float32)
        pre_grad = (hidden_grad * (normal_cdf + pre_act * normal_pdf)).astype(jnp.bfloat16)
        input_grads = jnp.dot(pre_grad, first_weight.T, preferred_element_type=jnp.float32).astype(jnp.bfloat16)
        first_part = jnp.einsum('grf,grd->gfd', pre_grad.reshape(N_DP, group, FF).astype(jnp.float32), rows_in.reshape(N_DP, group, D).astype(jnp.float32))
        first_part = lax.optimization_barrier(first_part.astype(jnp.bfloat16))
        first_total = jnp.sum(first_part, axis=0, dtype=jnp.float32).astype(jnp.bfloat16)
        second_part = jnp.einsum('grf,grd->gfd', hidden.reshape(N_DP, group, FF).astype(jnp.float32), rows_cotan.reshape(N_DP, group, D).astype(jnp.float32))
        second_part = lax.optimization_barrier(second_part.astype(jnp.bfloat16))
        second_total = jnp.sum(second_part, axis=0, dtype=jnp.float32).astype(jnp.bfloat16)
        return outputs, input_grads, first_total, second_total

    slot_outputs, input_grads, first_totals, second_totals = lax.map(expert_pass, (inputs_by_expert, cotan_by_expert, in_weights, out_weights))
    out_blocks = jnp.swapaxes(slot_outputs, 0, 1).reshape(N_DP, group, EXPERTS, D)
    grad_blocks = jnp.swapaxes(input_grads, 0, 1).reshape(N_DP, group, EXPERTS, D)

    def token_pass(items):
        images, grads, outputs, slot_grads = items
        dispatch, combine = probabilities(images, router)
        combine_grad = jnp.einsum('bpd,bsd->bsp', grads.astype(jnp.float32), outputs.astype(jnp.float32))
        dispatch_grad = jnp.einsum('bpd,bsd->bsp', images.astype(jnp.float32), slot_grads.astype(jnp.float32))
        logit_grad = combine * (combine_grad - jnp.sum(combine * combine_grad, axis=1, keepdims=True))
        logit_grad = logit_grad + dispatch * (dispatch_grad - jnp.sum(dispatch * dispatch_grad, axis=2, keepdims=True))
        logit_low = lowered(logit_grad)
        token_grad = jnp.einsum('bsp,bsd->bpd', lowered(dispatch), slot_grads.astype(jnp.float32))
        token_grad = token_grad + jnp.einsum('bsp,ds->bpd', logit_low, router.astype(jnp.float32))
        router_part = jnp.einsum('bpd,bsp->ds', images.astype(jnp.float32), logit_low)
        return token_grad.astype(jnp.bfloat16), router_part

    token_grads, router_parts = lax.map(token_pass, (tok_blocks, cot_blocks, out_blocks, grad_blocks))
    router_grad = jnp.sum(router_parts, axis=0)
    in_weight_grad = jnp.transpose(first_totals, (1, 0, 2))
    out_weight_grad = jnp.transpose(second_totals, (1, 0, 2))
    return token_grads.reshape(IMAGES, PATCHES, D), router_grad, in_weight_grad, out_weight_grad
```

```python
import functools

import jax
import jax.numpy as jnp
from jax import lax
from jax.experimental import pallas as pl
from jax.experimental.pallas import tpu as pltpu
from jax.sharding import PartitionSpec as P

MESH = pl.DeviceIdType.MESH
LOW = jnp.bfloat16
F32 = jnp.float32
QUAD = 4
LANES = 128
ROWS = 16
half_root = 0.7071067811865476
inv_root_two_pi = 0.3989422804014327


def dot(a, b, dims):
    return lax.dot_general(a, b, (dims, ((), ())), preferred_element_type=F32)


NN = ((1,), (0,))
NT = ((1,), (1,))
TN = ((0,), (0,))


def pack(stage, dst, first, second):
    slots, width = first.shape
    parts = width // LANES
    for i, value in enumerate((first, second)):
        for j in range(parts):
            stage[pl.ds(i * parts + j, slots, stride=ROWS), :] = value[:, j * LANES : (j + 1) * LANES]
    dst[...] = stage[...].reshape(slots, ROWS, LANES).astype(LOW)


def unpack(stage, src, width):
    slots = src.shape[0]
    parts = width // LANES
    stage[...] = src[...].astype(F32).reshape(slots * ROWS, LANES)
    both = []
    for i in range(2):
        columns = [stage[pl.ds(i * parts + j, slots, stride=ROWS), :] for j in range(parts)]
        both.append(jnp.concatenate(columns, axis=1).astype(LOW))
    return both


def kernel(
    n_dp, n_e,
    tok_h, cot_h, rt_h, w1_h, w2_h,
    tg_h, rg_h, gw_h,
    tok, cot, rt, w1, w2, stage, stage_b,
    s1, r1, s2, r2, rows, msgs, part, total,
    tiles, tiles_in, sum_x, sum_q, tiles_out,
    core_out, core_in, pair_out, pair_in,
    tg, rg, gw,
    load, store, send, recv,
):
    dp, e = lax.axis_index("dp"), lax.axis_index("expert")
    n_x = n_dp // QUAD
    x, q = dp // QUAD, lax.rem(dp, QUAD)
    slots = n_e
    width = tok.shape[1]
    ff = w1.shape[1]
    share = ff // n_dp
    n_tiles = tiles.shape[0]
    tile_rows = tiles.shape[1]
    across = width // LANES

    loads = [
        pltpu.make_async_copy(src, dst, load.at[i])
        for i, (src, dst) in enumerate(((rt_h, rt), (tok_h, tok), (cot_h, cot), (w1_h, w1), (w2_h, w2)))
    ]
    for copy in loads:
        copy.start()
    stage[...] = jnp.zeros_like(stage)

    barrier = pltpu.get_barrier_semaphore()

    def greet(device):
        pl.semaphore_signal(barrier, inc=1, device_id=device, device_id_type=MESH)

    @pl.loop(1, n_e)
    def _(o):
        greet((dp, lax.rem(e + o, n_e)))

    @pl.loop(1, n_x)
    def _(o):
        greet((lax.rem(x + o, n_x) * QUAD + q, e))

    for o in range(1, QUAD):
        greet((x * QUAD + lax.rem(q + o, QUAD), e))

    def remote(src, dst, at, device):
        return pltpu.make_async_remote_copy(
            src_ref=src, dst_ref=dst, send_sem=send.at[at], recv_sem=recv.at[at],
            device_id=device, device_id_type=MESH,
        )

    next_e = (dp, lax.rem(e + 1, n_e))
    next_x = (lax.rem(x + 1, n_x) * QUAD + q, e)
    next_q = (x * QUAD + lax.rem(q + 1, QUAD), e)

    def all_of(ref, count, at, device):
        return remote(ref.at[pl.ds(0, count)], ref.at[pl.ds(0, count)], at, device)

    loads[0].wait()
    loads[1].wait()
    logits = dot(rt[...], tok[...], NT)
    over_patches = jnp.exp(logits - jnp.max(logits, axis=1, keepdims=True))
    dispatch = over_patches / jnp.sum(over_patches, axis=1, keepdims=True)
    over_slots = jnp.exp(logits - jnp.max(logits, axis=0, keepdims=True))
    combine = over_slots / jnp.sum(over_slots, axis=0, keepdims=True)
    dispatch_low = dispatch.astype(LOW)
    combine_low = combine.astype(LOW)
    slot_inputs = dot(dispatch_low, tok[...], NN)
    loads[2].wait()
    slot_cotan = dot(combine_low, cot[...], NN)
    pack(stage, s1, slot_inputs, slot_cotan)
    pl.semaphore_wait(barrier, n_e - 1 + n_x - 1 + QUAD - 1)

    @pl.loop(1, n_e)
    def _(o):
        peer = lax.rem(e + o, n_e)
        remote(s1.at[peer], r1.at[e], 0, (dp, peer)).start()

    r1[e] = s1[e]
    all_of(r1, n_e - 1, 0, next_e).wait_recv()

    rows_in, rows_cotan = unpack(stage_b, r1, width)
    rows[x, 0] = rows_in
    rows[x, 1] = rows_cotan

    @pl.loop(1, n_x)
    def _(o):
        peer = lax.rem(x + o, n_x)
        remote(rows.at[x], rows.at[x], 1, (peer * QUAD + q, e)).start()

    loads[3].wait()
    loads[4].wait()
    block = ff // n_x
    pair = 2 * block
    per = 2 if ff % (2 * pair) == 0 else 1
    step = per * pair
    outputs = jnp.zeros((slots, width), F32)
    grads = jnp.zeros((slots, width), F32)
    is_first = lax.broadcasted_iota(jnp.int32, (slots, pair), 1) < block
    for k in range(ff // step):
        first = w1[:, k * step : (k + 1) * step]
        second = w2[k * step : (k + 1) * step, :]
        pre_act = dot(rows_in, first, NN)
        hidden_grad = dot(rows_cotan, second, NT)
        normal_cdf = 0.5 * (1.0 + lax.erf(pre_act * half_root))
        normal_pdf = jnp.exp(-0.5 * pre_act * pre_act) * inv_root_two_pi
        hidden = pre_act * normal_cdf
        pre_grad = hidden_grad * (normal_cdf + pre_act * normal_pdf)
        outputs += dot(hidden.astype(LOW), second, NN)
        grads += dot(pre_grad.astype(LOW), first, NT)
        for i in range(per):
            p_part = pre_grad[:, i * pair : (i + 1) * pair]
            h_part = hidden[:, i * pair : (i + 1) * pair]
            at = 2 * (k * per + i)
            msgs[at] = jnp.where(is_first, p_part, pltpu.roll(h_part, block, 1)).astype(LOW)
            msgs[at + 1] = jnp.where(is_first, pltpu.roll(p_part, block, 1), h_part).astype(LOW)
    pack(stage, s2, outputs, grads)

    @pl.loop(1, n_e)
    def _(o):
        peer = lax.rem(e + o, n_e)
        remote(s2.at[peer], r2.at[e], 2, (dp, peer)).start()

    @pl.loop(1, n_x)
    def _(o):
        peer = lax.rem(x + o, n_x)
        remote(msgs.at[peer], part.at[x], 3, (peer * QUAD + q, e)).start()

    part[x] = msgs[x]
    r2[e] = s2[e]
    all_of(r2, n_e - 1, 2, next_e).wait_recv()

    slot_outputs, input_grads = unpack(stage_b, r2, width)
    combine_grad = dot(slot_outputs, cot[...], NT)
    dispatch_grad = dot(input_grads, tok[...], NT)
    logit_grad = combine * (combine_grad - jnp.sum(combine * combine_grad, axis=0, keepdims=True))
    logit_grad += dispatch * (dispatch_grad - jnp.sum(dispatch * dispatch_grad, axis=1, keepdims=True))
    logit_low = logit_grad.astype(LOW)
    router_part = dot(logit_low, tok[...], NN)
    for t in range(n_tiles):
        i, j = divmod(t, across)
        tiles[t] = router_part[i * tile_rows : (i + 1) * tile_rows, j * LANES : (j + 1) * LANES]

    @pl.loop(1, n_e)
    def _(o):
        peer = lax.rem(e + o, n_e)

        @pl.when(peer < n_tiles)
        def _():
            remote(tiles.at[peer], tiles_in.at[e], 4, (dp, peer)).start()

    weights = jnp.concatenate([dispatch_low, logit_low], axis=0)
    values = jnp.concatenate([input_grads, rt[...]], axis=0)
    tg[...] = dot(weights, values, TN).astype(LOW)
    tg_copy = pltpu.make_async_copy(tg, tg_h, store.at[0])
    tg_copy.start()

    @pl.when(e < n_tiles)
    def _():
        tiles_in[e] = tiles[e]
        all_of(tiles_in, n_e - 1, 4, next_e).wait_recv()
        sum_x[x] = jnp.sum(tiles_in[...], axis=0)

        @pl.loop(1, n_x)
        def _(o):
            peer = lax.rem(x + o, n_x)
            remote(sum_x.at[x], sum_x.at[x], 5, (peer * QUAD + q, e)).start()

        all_of(sum_x, n_x - 1, 5, next_x).wait_recv()
        sum_q[q] = jnp.sum(sum_x[...], axis=0)
        for o in range(1, QUAD):
            remote(sum_q.at[q], sum_q.at[q], 6, (x * QUAD + lax.rem(q + o, QUAD), e)).start()
        all_of(sum_q, QUAD - 1, 6, next_q).wait_recv()
        tiles_out[e] = jnp.sum(sum_q[...], axis=0)

        @pl.loop(1, n_e)
        def _(o):
            peer = lax.rem(e + o, n_e)
            remote(tiles_out.at[e], tiles_out.at[e], 7, (dp, peer)).start()

    all_of(rows, n_x - 1, 1, next_x).wait_recv()
    all_of(part, n_x - 1, 3, next_x).wait_recv()
    left = part[...].reshape(n_x * slots, pair).T
    for i in range(2):
        total[i] = dot(left[i * block : (i + 1) * block], rows[:, i].reshape(n_x * slots, width), NN).reshape(QUAD, share, width)
    z, core = q // 2, lax.rem(q, 2)
    for i in range(2):
        for there in range(2):
            core_out[there, i] = total[i, there * 2 + 1 - core].astype(LOW)
    core_copy = remote(core_out, core_in, 8, (x * QUAD + z * 2 + 1 - core, e))
    core_copy.start()
    core_copy.wait_recv()
    for i in range(2):
        pair_out[i] = (total[i, (1 - z) * 2 + core] + core_in[1 - z, i].astype(F32)).astype(LOW)
    pair_copy = remote(pair_out, pair_in, 9, (x * QUAD + (1 - z) * 2 + core, e))
    pair_copy.start()

    @pl.when(e < n_tiles)
    def _():
        all_of(tiles_out, n_tiles - 1, 7, next_e).wait_recv()

    @pl.when(e >= n_tiles)
    def _():
        all_of(tiles_out, n_tiles, 7, next_e).wait_recv()

    for t in range(n_tiles):
        i, j = divmod(t, across)
        rg[i * tile_rows : (i + 1) * tile_rows, j * LANES : (j + 1) * LANES] = tiles_out[t]
    rg_copy = pltpu.make_async_copy(rg, rg_h, store.at[1])
    rg_copy.start()

    pair_copy.wait_recv()
    for i in range(2):
        gw[i] = (total[i, q] + core_in[z, i].astype(F32) + pair_in[i].astype(F32)).astype(LOW)
    gw_copy = pltpu.make_async_copy(gw, gw_h, store.at[2])
    gw_copy.start()

    all_of(s1, n_e - 1, 0, next_e).wait_send()
    all_of(rows, n_x - 1, 1, next_x).wait_send()
    all_of(s2, n_e - 1, 2, next_e).wait_send()
    all_of(msgs, n_x - 1, 3, next_x).wait_send()
    core_copy.wait_send()
    pair_copy.wait_send()

    @pl.when(e < n_tiles)
    def _():
        all_of(tiles, n_tiles - 1, 4, next_e).wait_send()
        all_of(sum_x, n_x - 1, 5, next_x).wait_send()
        all_of(sum_q, QUAD - 1, 6, next_q).wait_send()
        all_of(tiles_in, n_e - 1, 7, next_e).wait_send()

    @pl.when(e >= n_tiles)
    def _():
        all_of(tiles, n_tiles, 4, next_e).wait_send()

    tg_copy.wait()
    rg_copy.wait()
    gw_copy.wait()


def on_device(n_dp, n_e, tokens, cotangent, router, in_weights, out_weights):
    _, patches, width = tokens.shape
    ff = in_weights.shape[2]
    slots = router.shape[1]
    n_x = n_dp // QUAD
    share = ff // n_dp
    tile_rows = min(8, slots)
    n_tiles = slots // tile_rows * (width // LANES)
    vmem = pltpu.VMEM
    dma = pltpu.SemaphoreType.DMA
    token_grad, router_grad, weight_grads = pl.pallas_call(
        functools.partial(kernel, n_dp, n_e),
        out_shape=(
            jax.ShapeDtypeStruct((patches, width), LOW),
            jax.ShapeDtypeStruct((slots, width), F32),
            jax.ShapeDtypeStruct((2, share, width), LOW),
        ),
        in_specs=[pl.BlockSpec(memory_space=pl.ANY)] * 5,
        out_specs=[pl.BlockSpec(memory_space=pl.ANY)] * 3,
        scratch_shapes=[
            vmem((patches, width), LOW),
            vmem((patches, width), LOW),
            vmem((slots, width), LOW),
            vmem((width, ff), LOW),
            vmem((ff, width), LOW),
            vmem((slots * ROWS, LANES), F32),
            vmem((slots * ROWS, LANES), F32),
            *[vmem((slots, ROWS, LANES), LOW)] * 4,
            vmem((n_x, 2, slots, width), LOW),
            vmem((n_x, slots, 2 * ff // n_x), LOW),
            vmem((n_x, slots, 2 * ff // n_x), LOW),
            vmem((2, QUAD, share, width), F32),
            vmem((n_tiles, tile_rows, LANES), F32),
            vmem((n_e, tile_rows, LANES), F32),
            vmem((n_x, tile_rows, LANES), F32),
            vmem((QUAD, tile_rows, LANES), F32),
            vmem((n_tiles, tile_rows, LANES), F32),
            vmem((2, 2, share, width), LOW),
            vmem((2, 2, share, width), LOW),
            vmem((2, share, width), LOW),
            vmem((2, share, width), LOW),
            vmem((patches, width), LOW),
            vmem((slots, width), F32),
            vmem((2, share, width), LOW),
            dma((5,)),
            dma((3,)),
            dma((10,)),
            dma((10,)),
        ],
        compiler_params=pltpu.CompilerParams(
            collective_id=0, has_side_effects=True, vmem_limit_bytes=56 * 2**20
        ),
        cost_estimate=pl.CostEstimate(flops=10**9, bytes_accessed=10**7, transcendentals=10**5),
    )(tokens[0], cotangent[0], router.T, in_weights[0], out_weights[0])
    return (
        token_grad[None],
        router_grad.T,
        weight_grads[0][:, None],
        weight_grads[1][:, None],
    )


def solution(mesh):
    image = P(("dp", "expert"), None, None)
    expert = P("expert", None, None)
    grad = P("dp", "expert", None)
    return jax.shard_map(
        functools.partial(on_device, mesh.shape["dp"], mesh.shape["expert"]),
        mesh=mesh,
        in_specs=(image, image, P(), expert, expert),
        out_specs=(image, P(), grad, grad),
        check_vma=False,
    )
```

```python
import functools

import jax
import jax.numpy as jnp
from jax import lax
from jax.experimental import pallas as pl
from jax.experimental.pallas import tpu as pltpu
from jax.sharding import PartitionSpec as P

MESH = pl.DeviceIdType.MESH
LOW = jnp.bfloat16
F32 = jnp.float32
QUAD = 4
LANES = 128
ROWS = 16
half_root = 0.7071067811865476
inv_root_two_pi = 0.3989422804014327


def dot(a, b, dims):
    return lax.dot_general(a, b, (dims, ((), ())), preferred_element_type=F32)


NN = ((1,), (0,))
NT = ((1,), (1,))
TN = ((0,), (0,))


def pack(stage, dst, first, second):
    slots, width = first.shape
    parts = width // LANES
    for i, value in enumerate((first, second)):
        for j in range(parts):
            stage[pl.ds(i * parts + j, slots, stride=ROWS), :] = value[:, j * LANES : (j + 1) * LANES]
    dst[...] = stage[...].reshape(slots, ROWS, LANES).astype(LOW)


def unpack(stage, src, width):
    slots = src.shape[0]
    parts = width // LANES
    stage[...] = src[...].astype(F32).reshape(slots * ROWS, LANES)
    both = []
    for i in range(2):
        columns = [stage[pl.ds(i * parts + j, slots, stride=ROWS), :] for j in range(parts)]
        both.append(jnp.concatenate(columns, axis=1).astype(LOW))
    return both


def kernel(
    n_dp, n_e,
    tok_h, cot_h, rt_h, w1_h, w2_h,
    tg, rg, g1, g2,
    tok, cot, rt, w1, w2, stage, stage_b,
    s1, r1, s2, r2, rows, msgs, part, total,
    tiles, tiles_in, sum_e, tiles_out,
    core_out, core_in, pair_out, pair_in,
    load, send, recv, ring_send, ring_recv,
):
    dp, e = lax.axis_index("dp"), lax.axis_index("expert")
    n_x = n_dp // QUAD
    x, q = dp // QUAD, lax.rem(dp, QUAD)
    slots = n_e
    width = tok.shape[1]
    ff = w1.shape[1]
    share = ff // n_dp
    n_tiles = tiles.shape[0]
    tile_rows = tiles.shape[1]
    across = width // LANES

    loads = [
        pltpu.make_async_copy(src, dst, load.at[i])
        for i, (src, dst) in enumerate(((rt_h, rt), (tok_h, tok), (cot_h, cot), (w1_h, w1), (w2_h, w2)))
    ]
    for copy in loads:
        copy.start()
    stage[...] = jnp.zeros_like(stage)

    def each(count, body):
        far = max(1, count * 3 // 8)
        for o in (*range(far, count), *range(1, far)):
            body(o)

    def to_experts(body):
        each(n_e, lambda o: body(lax.rem(e + o, n_e)))

    def to_replicas(body):
        each(n_dp, lambda o: body(lax.rem(dp + o, n_dp)))

    barrier = pltpu.get_barrier_semaphore()

    def greet(device):
        pl.semaphore_signal(barrier, inc=1, device_id=device, device_id_type=MESH)

    to_experts(lambda peer: greet((dp, peer)))
    to_replicas(lambda peer: greet((peer, e)))

    def remote(src, dst, at, device):
        return pltpu.make_async_remote_copy(
            src_ref=src, dst_ref=dst, send_sem=send.at[at], recv_sem=recv.at[at],
            device_id=device, device_id_type=MESH,
        )

    next_e = (dp, lax.rem(e + 1, n_e))
    next_x = (lax.rem(x + 1, n_x) * QUAD + q, e)
    next_dp = (lax.rem(dp + 1, n_dp), e)

    half = n_x // 2
    right = next_x
    left = (lax.rem(x + n_x - 1, n_x) * QUAD + q, e)

    def ring(s, sender):
        a = lax.rem(x - (s - 1 + sender) + n_x, n_x)
        b = lax.rem(x + s - 1 + sender, n_x)
        blocks = (rows.at[a], rows.at[b]) if s < half else (rows.at[a, 0], rows.at[b, 1])
        return [
            pltpu.make_async_remote_copy(
                src_ref=block, dst_ref=block, send_sem=ring_send.at[s - 1, i], recv_sem=ring_recv.at[s - 1, i],
                device_id=device, device_id_type=MESH,
            )
            for i, (block, device) in enumerate(zip(blocks, (right, left)))
        ]

    def ring_start(s):
        for copy in ring(s, 0):
            copy.start()

    def ring_arrived(s):
        for copy in ring(s, 1):
            copy.wait_recv()

    def all_of(ref, count, at, device):
        return remote(ref.at[pl.ds(0, count)], ref.at[pl.ds(0, count)], at, device)

    loads[0].wait()
    loads[1].wait()
    logits = dot(rt[...], tok[...], NT)
    over_patches = jnp.exp(logits - jnp.max(logits, axis=1, keepdims=True))
    dispatch = over_patches / jnp.sum(over_patches, axis=1, keepdims=True)
    over_slots = jnp.exp(logits - jnp.max(logits, axis=0, keepdims=True))
    combine = over_slots / jnp.sum(over_slots, axis=0, keepdims=True)
    dispatch_low = dispatch.astype(LOW)
    combine_low = combine.astype(LOW)
    slot_inputs = dot(dispatch_low, tok[...], NN)
    loads[2].wait()
    slot_cotan = dot(combine_low, cot[...], NN)
    pack(stage, s1, slot_inputs, slot_cotan)
    pl.semaphore_wait(barrier, n_e - 1 + n_dp - 1)

    @to_experts
    def _(peer):
        remote(s1.at[peer], r1.at[e], 0, (dp, peer)).start()

    r1[e] = s1[e]
    all_of(r1, n_e - 1, 0, next_e).wait_recv()

    rows_in, rows_cotan = unpack(stage_b, r1, width)
    rows[x, 0] = rows_in
    rows[x, 1] = rows_cotan

    ring_start(1)

    loads[3].wait()
    loads[4].wait()
    block = ff // n_x
    pair = 2 * block
    per = 2 if ff % (2 * pair) == 0 else 1
    step = per * pair
    outputs = jnp.zeros((slots, width), F32)
    grads = jnp.zeros((slots, width), F32)
    is_first = lax.broadcasted_iota(jnp.int32, (slots, pair), 1) < block
    for k in range(ff // step):
        first = w1[:, k * step : (k + 1) * step]
        second = w2[k * step : (k + 1) * step, :]
        pre_act = dot(rows_in, first, NN)
        hidden_grad = dot(rows_cotan, second, NT)
        normal_cdf = 0.5 * (1.0 + lax.erf(pre_act * half_root))
        normal_pdf = jnp.exp(-0.5 * pre_act * pre_act) * inv_root_two_pi
        hidden = pre_act * normal_cdf
        pre_grad = hidden_grad * (normal_cdf + pre_act * normal_pdf)
        outputs += dot(hidden.astype(LOW), second, NN)
        grads += dot(pre_grad.astype(LOW), first, NT)
        for i in range(per):
            p_part = pre_grad[:, i * pair : (i + 1) * pair]
            h_part = hidden[:, i * pair : (i + 1) * pair]
            at = 2 * (k * per + i)
            msgs[at] = jnp.where(is_first, p_part, pltpu.roll(h_part, block, 1)).astype(LOW)
            msgs[at + 1] = jnp.where(is_first, pltpu.roll(p_part, block, 1), h_part).astype(LOW)
    pack(stage, s2, outputs, grads)

    @to_experts
    def _(peer):
        remote(s2.at[peer], r2.at[e], 2, (dp, peer)).start()

    @functools.partial(each, n_x)
    def _(o):
        peer = lax.rem(x + o, n_x)
        remote(msgs.at[peer], part.at[x], 3, (peer * QUAD + q, e)).start()

    part[x] = msgs[x]
    r2[e] = s2[e]
    for s in range(1, half):
        ring_arrived(s)
        ring_start(s + 1)
    all_of(r2, n_e - 1, 2, next_e).wait_recv()

    slot_outputs, input_grads = unpack(stage_b, r2, width)
    combine_grad = dot(slot_outputs, cot[...], NT)
    dispatch_grad = dot(input_grads, tok[...], NT)
    logit_grad = combine * (combine_grad - jnp.sum(combine * combine_grad, axis=0, keepdims=True))
    logit_grad += dispatch * (dispatch_grad - jnp.sum(dispatch * dispatch_grad, axis=1, keepdims=True))
    logit_low = logit_grad.astype(LOW)
    router_part = dot(logit_low, tok[...], NN)
    for t in range(n_tiles):
        i, j = divmod(t, across)
        tiles[t] = router_part[i * tile_rows : (i + 1) * tile_rows, j * LANES : (j + 1) * LANES]

    @to_replicas
    def _(peer):
        @pl.when(peer < n_tiles)
        def _():
            remote(tiles.at[peer], tiles_in.at[dp], 4, (peer, e)).start()

    weights = jnp.concatenate([dispatch_low, logit_low], axis=0)
    values = jnp.concatenate([input_grads, rt[...]], axis=0)
    tg[...] = dot(weights, values, TN).astype(LOW)

    ring_arrived(half)
    all_of(part, n_x - 1, 3, next_x).wait_recv()
    wide = part[...].reshape(n_x * slots, pair).T
    z, core = q // 2, lax.rem(q, 2)
    other_core = (x * QUAD + z * 2 + 1 - core, e)
    other_pair = (x * QUAD + (1 - z) * 2 + core, e)
    blocks = ((1 - z) * 2, z * 2)
    core_copies = [[remote(core_out.at[k, i], core_in.at[k, i], 8 + 2 * k + i, other_core) for i in range(2)] for k in range(2)]
    pair_copies = [remote(pair_out.at[i], pair_in.at[i], 12 + i, other_pair) for i in range(2)]
    for i in range(2):
        values = rows[:, i].reshape(n_x * slots, width)
        total[i] = dot(wide[i * block : (i + 1) * block], values, NN).reshape(QUAD, share, width)
        core_out[0, i] = total[i, blocks[0] + 1 - core].astype(LOW)
        core_copies[0][i].start()
    for i in range(2):
        core_out[1, i] = total[i, blocks[1] + 1 - core].astype(LOW)
        core_copies[1][i].start()

    @pl.when(dp < n_tiles)
    def _():
        tiles_in[dp] = tiles[dp]
        all_of(tiles_in, n_dp - 1, 4, next_dp).wait_recv()
        sum_e[e] = jnp.sum(tiles_in[...], axis=0)

        @to_experts
        def _(peer):
            remote(sum_e.at[e], sum_e.at[e], 5, (dp, peer)).start()

    for i in range(2):
        core_copies[0][i].wait_recv()
        pair_out[i] = (total[i, blocks[0] + core] + core_in[0, i].astype(F32)).astype(LOW)
        pair_copies[i].start()

    @pl.when(dp < n_tiles)
    def _():
        all_of(sum_e, n_e - 1, 5, next_e).wait_recv()
        tiles_out[dp] = jnp.sum(sum_e[...], axis=0)

        @to_replicas
        def _(peer):
            remote(tiles_out.at[dp], tiles_out.at[dp], 6, (peer, e)).start()

    for i, out in enumerate((g1, g2)):
        core_copies[1][i].wait_recv()
        pair_copies[i].wait_recv()
        out[...] = (total[i, q] + core_in[1, i].astype(F32) + pair_in[i].astype(F32)).astype(LOW)

    @pl.when(dp < n_tiles)
    def _():
        all_of(tiles_out, n_tiles - 1, 6, next_dp).wait_recv()

    @pl.when(dp >= n_tiles)
    def _():
        all_of(tiles_out, n_tiles, 6, next_dp).wait_recv()

    for t in range(n_tiles):
        i, j = divmod(t, across)
        rg[i * tile_rows : (i + 1) * tile_rows, j * LANES : (j + 1) * LANES] = tiles_out[t]

    all_of(s1, n_e - 1, 0, next_e).wait_send()
    for s in range(1, half + 1):
        for copy in ring(s, 0):
            copy.wait_send()
    all_of(s2, n_e - 1, 2, next_e).wait_send()
    all_of(msgs, n_x - 1, 3, next_x).wait_send()
    for copy in core_copies[0] + core_copies[1] + pair_copies:
        copy.wait_send()

    @pl.when(dp < n_tiles)
    def _():
        all_of(tiles, n_tiles - 1, 4, next_dp).wait_send()
        all_of(sum_e, n_e - 1, 5, next_e).wait_send()
        all_of(tiles_in, n_dp - 1, 6, next_dp).wait_send()

    @pl.when(dp >= n_tiles)
    def _():
        all_of(tiles, n_tiles, 4, next_dp).wait_send()


def deliver(*refs):
    count = len(refs) // 2
    sems = refs[-1]
    copies = [pltpu.make_async_copy(refs[i], refs[count + i], sems.at[i]) for i in range(count)]
    for copy in copies:
        copy.start()
    for copy in copies:
        copy.wait()


def on_device(n_dp, n_e, tokens, cotangent, router, in_weights, out_weights):
    _, patches, width = tokens.shape
    ff = in_weights.shape[2]
    slots = router.shape[1]
    n_x = n_dp // QUAD
    share = ff // n_dp
    tile_rows = min(8, slots)
    n_tiles = slots // tile_rows * (width // LANES)
    vmem = pltpu.VMEM
    dma = pltpu.SemaphoreType.DMA
    shapes = (
        ((patches, width), LOW),
        ((slots, width), F32),
        ((share, width), LOW),
        ((share, width), LOW),
    )
    results = pl.pallas_call(
        functools.partial(kernel, n_dp, n_e),
        out_shape=[vmem(*shape) for shape in shapes],
        in_specs=[pl.BlockSpec(memory_space=pl.ANY)] * 5,
        out_specs=[pl.BlockSpec(memory_space=vmem)] * 4,
        scratch_shapes=[
            vmem((patches, width), LOW),
            vmem((patches, width), LOW),
            vmem((slots, width), LOW),
            vmem((width, ff), LOW),
            vmem((ff, width), LOW),
            vmem((slots * ROWS, LANES), F32),
            vmem((slots * ROWS, LANES), F32),
            *[vmem((slots, ROWS, LANES), LOW)] * 4,
            vmem((n_x, 2, slots, width), LOW),
            vmem((n_x, slots, 2 * ff // n_x), LOW),
            vmem((n_x, slots, 2 * ff // n_x), LOW),
            vmem((2, QUAD, share, width), F32),
            vmem((n_tiles, tile_rows, LANES), F32),
            vmem((n_dp, tile_rows, LANES), F32),
            vmem((n_e, tile_rows, LANES), F32),
            vmem((n_tiles, tile_rows, LANES), F32),
            vmem((2, 2, share, width), LOW),
            vmem((2, 2, share, width), LOW),
            vmem((2, share, width), LOW),
            vmem((2, share, width), LOW),
            dma((5,)),
            dma((14,)),
            dma((14,)),
            dma((n_x // 2, 2)),
            dma((n_x // 2, 2)),
        ],
        compiler_params=pltpu.CompilerParams(
            collective_id=0, has_side_effects=True, vmem_limit_bytes=56 * 2**20
        ),
        cost_estimate=pl.CostEstimate(flops=10**9, bytes_accessed=10**7, transcendentals=10**5),
    )(tokens[0], cotangent[0], router.T, in_weights[0], out_weights[0])
    token_grad, router_grad, in_grad, out_grad = pl.pallas_call(
        deliver,
        out_shape=[jax.ShapeDtypeStruct(*shape) for shape in shapes],
        in_specs=[pl.BlockSpec(memory_space=vmem)] * 4,
        out_specs=[pl.BlockSpec(memory_space=pl.ANY)] * 4,
        scratch_shapes=[dma((4,))],
    )(*[pltpu.with_memory_space_constraint(result, vmem) for result in results])
    return token_grad[None], router_grad.T, in_grad[:, None], out_grad[:, None]


def solution(mesh):
    image = P(("dp", "expert"), None, None)
    expert = P("expert", None, None)
    grad = P("dp", "expert", None)
    return jax.shard_map(
        functools.partial(on_device, mesh.shape["dp"], mesh.shape["expert"]),
        mesh=mesh,
        in_specs=(image, image, P(), expert, expert),
        out_specs=(image, P(), grad, grad),
        check_vma=False,
    )
```

```python
import functools

import jax
import jax.numpy as jnp
from jax import lax
from jax.experimental import pallas as pl
from jax.experimental.pallas import tpu as pltpu
from jax.sharding import PartitionSpec as P

MESH = pl.DeviceIdType.MESH
LOW = jnp.bfloat16
F32 = jnp.float32
QUAD = 4
LANES = 128
ROWS = 16
half_root = 0.7071067811865476
inv_root_two_pi = 0.3989422804014327


def dot(a, b, dims):
    return lax.dot_general(a, b, (dims, ((), ())), preferred_element_type=F32)


NN = ((1,), (0,))
NT = ((1,), (1,))
TN = ((0,), (0,))


def pack(stage, dst, first, second):
    slots, width = first.shape
    parts = width // LANES
    for i, value in enumerate((first, second)):
        for j in range(parts):
            stage[pl.ds(i * parts + j, slots, stride=ROWS), :] = value[:, j * LANES : (j + 1) * LANES]
    dst[...] = stage[...].reshape(slots, ROWS, LANES).astype(LOW)


def unpack(stage, src, width):
    slots = src.shape[0]
    parts = width // LANES
    stage[...] = src[...].astype(F32).reshape(slots * ROWS, LANES)
    both = []
    for i in range(2):
        columns = [stage[pl.ds(i * parts + j, slots, stride=ROWS), :] for j in range(parts)]
        both.append(jnp.concatenate(columns, axis=1).astype(LOW))
    return both


def kernel(
    n_dp, n_e,
    tok_h, cot_h, rt_h, w1_h, w2_h,
    tg, rg, g1, g2,
    tok, cot, rt, w1, w2, stage, stage_b,
    s1, r1, s2, r2, rows, msgs, part, total,
    tiles, tiles_in, sum_e, tiles_out,
    core_out, core_in, pair_out, pair_in,
    load, send, recv, ring_send, ring_recv,
):
    dp, e = lax.axis_index("dp"), lax.axis_index("expert")
    n_x = n_dp // QUAD
    x, q = dp // QUAD, lax.rem(dp, QUAD)
    slots = n_e
    width = tok.shape[1]
    ff = w1.shape[1]
    share = ff // n_dp
    n_tiles = tiles.shape[0]
    tile_rows = tiles.shape[1]
    across = width // LANES

    def each(count, body):
        far = max(1, count * 3 // 8)
        for o in (*range(far, count), *range(1, far)):
            body(o)

    def to_experts(body):
        each(n_e, lambda o: body(lax.rem(e + o, n_e)))

    def to_replicas(body):
        each(n_dp, lambda o: body(lax.rem(dp + o, n_dp)))

    barrier = pltpu.get_barrier_semaphore()

    def greet(device):
        pl.semaphore_signal(barrier, inc=1, device_id=device, device_id_type=MESH)

    to_experts(lambda peer: greet((dp, peer)))
    to_replicas(lambda peer: greet((peer, e)))

    loads = [
        pltpu.make_async_copy(src, dst, load.at[i])
        for i, (src, dst) in enumerate(((rt_h, rt), (tok_h, tok), (cot_h, cot), (w1_h, w1), (w2_h, w2)))
    ]
    for copy in loads:
        copy.start()
    stage[...] = jnp.zeros_like(stage)

    def remote(src, dst, at, device):
        return pltpu.make_async_remote_copy(
            src_ref=src, dst_ref=dst, send_sem=send.at[at], recv_sem=recv.at[at],
            device_id=device, device_id_type=MESH,
        )

    next_e = (dp, lax.rem(e + 1, n_e))
    next_x = (lax.rem(x + 1, n_x) * QUAD + q, e)
    next_dp = (lax.rem(dp + 1, n_dp), e)

    half = n_x // 2
    right = next_x
    left = (lax.rem(x + n_x - 1, n_x) * QUAD + q, e)

    def ring(s, sender):
        a = lax.rem(x - (s - 1 + sender) + n_x, n_x)
        b = lax.rem(x + s - 1 + sender, n_x)
        blocks = (rows.at[a], rows.at[b]) if s < half else (rows.at[a, 0], rows.at[b, 1])
        return [
            pltpu.make_async_remote_copy(
                src_ref=block, dst_ref=block, send_sem=ring_send.at[s - 1, i], recv_sem=ring_recv.at[s - 1, i],
                device_id=device, device_id_type=MESH,
            )
            for i, (block, device) in enumerate(zip(blocks, (right, left)))
        ]

    def ring_start(s):
        for copy in ring(s, 0):
            copy.start()

    def ring_arrived(s):
        for copy in ring(s, 1):
            copy.wait_recv()

    def all_of(ref, count, at, device):
        return remote(ref.at[pl.ds(0, count)], ref.at[pl.ds(0, count)], at, device)

    loads[0].wait()
    loads[1].wait()
    logits = dot(rt[...], tok[...], NT)
    over_patches = jnp.exp(logits - jnp.max(logits, axis=1, keepdims=True))
    dispatch = over_patches / jnp.sum(over_patches, axis=1, keepdims=True)
    over_slots = jnp.exp(logits - jnp.max(logits, axis=0, keepdims=True))
    combine = over_slots / jnp.sum(over_slots, axis=0, keepdims=True)
    dispatch_low = dispatch.astype(LOW)
    combine_low = combine.astype(LOW)
    slot_inputs = dot(dispatch_low, tok[...], NN)
    loads[2].wait()
    slot_cotan = dot(combine_low, cot[...], NN)
    pack(stage, s1, slot_inputs, slot_cotan)
    pl.semaphore_wait(barrier, n_e - 1 + n_dp - 1)

    @to_experts
    def _(peer):
        remote(s1.at[peer], r1.at[e], 0, (dp, peer)).start()

    r1[e] = s1[e]
    all_of(r1, n_e - 1, 0, next_e).wait_recv()

    rows_in, rows_cotan = unpack(stage_b, r1, width)
    rows[x, 0] = rows_in
    rows[x, 1] = rows_cotan

    ring_start(1)

    loads[3].wait()
    loads[4].wait()
    block = ff // n_x
    pair = 2 * block
    per = 2 if ff % (2 * pair) == 0 else 1
    step = per * pair
    outputs = jnp.zeros((slots, width), F32)
    grads = jnp.zeros((slots, width), F32)
    is_first = lax.broadcasted_iota(jnp.int32, (slots, pair), 1) < block
    for k in range(ff // step):
        first = w1[:, k * step : (k + 1) * step]
        second = w2[k * step : (k + 1) * step, :]
        pre_act = dot(rows_in, first, NN)
        hidden_grad = dot(rows_cotan, second, NT)
        normal_cdf = 0.5 * (1.0 + lax.erf(pre_act * half_root))
        normal_pdf = jnp.exp(-0.5 * pre_act * pre_act) * inv_root_two_pi
        hidden = pre_act * normal_cdf
        pre_grad = hidden_grad * (normal_cdf + pre_act * normal_pdf)
        outputs += dot(hidden.astype(LOW), second, NN)
        grads += dot(pre_grad.astype(LOW), first, NT)
        for i in range(per):
            p_part = pre_grad[:, i * pair : (i + 1) * pair]
            h_part = hidden[:, i * pair : (i + 1) * pair]
            at = 2 * (k * per + i)
            msgs[at] = jnp.where(is_first, p_part, pltpu.roll(h_part, block, 1)).astype(LOW)
            msgs[at + 1] = jnp.where(is_first, pltpu.roll(p_part, block, 1), h_part).astype(LOW)
            for to in (at, at + 1):

                @pl.when(x != to)
                def _():
                    remote(msgs.at[to], part.at[x], 3, (to * QUAD + q, e)).start()
    pack(stage, s2, outputs, grads)

    @to_experts
    def _(peer):
        remote(s2.at[peer], r2.at[e], 2, (dp, peer)).start()

    part[x] = msgs[x]
    r2[e] = s2[e]
    for s in range(1, half - 1):
        ring_arrived(s)
        ring_start(s + 1)
    all_of(r2, n_e - 1, 2, next_e).wait_recv()

    slot_outputs, input_grads = unpack(stage_b, r2, width)
    combine_grad = dot(slot_outputs, cot[...], NT)
    dispatch_grad = dot(input_grads, tok[...], NT)
    logit_grad = combine * (combine_grad - jnp.sum(combine * combine_grad, axis=0, keepdims=True))
    logit_grad += dispatch * (dispatch_grad - jnp.sum(dispatch * dispatch_grad, axis=1, keepdims=True))
    logit_low = logit_grad.astype(LOW)
    router_part = dot(logit_low, tok[...], NN)
    for t in range(n_tiles):
        i, j = divmod(t, across)
        tiles[t] = router_part[i * tile_rows : (i + 1) * tile_rows, j * LANES : (j + 1) * LANES]

    @to_replicas
    def _(peer):
        @pl.when(peer < n_tiles)
        def _():
            remote(tiles.at[peer], tiles_in.at[dp], 4, (peer, e)).start()

    if half > 1:
        ring_arrived(half - 1)
        ring_start(half)
    weights = jnp.concatenate([dispatch_low, logit_low], axis=0)
    values = jnp.concatenate([input_grads, rt[...]], axis=0)
    tg[...] = dot(weights, values, TN).astype(LOW)

    @pl.when(dp < n_tiles)
    def _():
        tiles_in[dp] = tiles[dp]
        all_of(tiles_in, n_dp - 1, 4, next_dp).wait_recv()
        sum_e[e] = jnp.sum(tiles_in[...], axis=0)

        @to_experts
        def _(peer):
            remote(sum_e.at[e], sum_e.at[e], 5, (dp, peer)).start()

    ring_arrived(half)
    all_of(part, n_x - 1, 3, next_x).wait_recv()
    wide = part[...].reshape(n_x * slots, pair).T
    z, core = q // 2, lax.rem(q, 2)
    other_core = (x * QUAD + z * 2 + 1 - core, e)
    other_pair = (x * QUAD + (1 - z) * 2 + core, e)
    blocks = ((1 - z) * 2, z * 2)
    core_copies = [[remote(core_out.at[k, i], core_in.at[k, i], 8 + 2 * k + i, other_core) for i in range(2)] for k in range(2)]
    pair_copies = [remote(pair_out.at[i], pair_in.at[i], 12 + i, other_pair) for i in range(2)]
    for i in range(2):
        values = rows[:, i].reshape(n_x * slots, width)
        total[i] = dot(wide[i * block : (i + 1) * block], values, NN).reshape(QUAD, share, width)
        core_out[0, i] = total[i, blocks[0] + 1 - core].astype(LOW)
        core_copies[0][i].start()
    for i in range(2):
        core_out[1, i] = total[i, blocks[1] + 1 - core].astype(LOW)
        core_copies[1][i].start()

    for i in range(2):
        core_copies[0][i].wait_recv()
        pair_out[i] = (total[i, blocks[0] + core] + core_in[0, i].astype(F32)).astype(LOW)
        pair_copies[i].start()

    @pl.when(dp < n_tiles)
    def _():
        all_of(sum_e, n_e - 1, 5, next_e).wait_recv()
        tiles_out[dp] = jnp.sum(sum_e[...], axis=0)

        @to_replicas
        def _(peer):
            remote(tiles_out.at[dp], tiles_out.at[dp], 6, (peer, e)).start()

    for i, out in enumerate((g1, g2)):
        core_copies[1][i].wait_recv()
        pair_copies[i].wait_recv()
        out[...] = (total[i, q] + core_in[1, i].astype(F32) + pair_in[i].astype(F32)).astype(LOW)

    @pl.when(dp < n_tiles)
    def _():
        all_of(tiles_out, n_tiles - 1, 6, next_dp).wait_recv()

    @pl.when(dp >= n_tiles)
    def _():
        all_of(tiles_out, n_tiles, 6, next_dp).wait_recv()

    for t in range(n_tiles):
        i, j = divmod(t, across)
        rg[i * tile_rows : (i + 1) * tile_rows, j * LANES : (j + 1) * LANES] = tiles_out[t]

    all_of(s1, n_e - 1, 0, next_e).wait_send()
    for s in range(1, half + 1):
        for copy in ring(s, 0):
            copy.wait_send()
    all_of(s2, n_e - 1, 2, next_e).wait_send()
    all_of(msgs, n_x - 1, 3, next_x).wait_send()
    for copy in core_copies[0] + core_copies[1] + pair_copies:
        copy.wait_send()

    @pl.when(dp < n_tiles)
    def _():
        all_of(tiles, n_tiles - 1, 4, next_dp).wait_send()
        all_of(sum_e, n_e - 1, 5, next_e).wait_send()
        all_of(tiles_in, n_dp - 1, 6, next_dp).wait_send()

    @pl.when(dp >= n_tiles)
    def _():
        all_of(tiles, n_tiles, 4, next_dp).wait_send()


def deliver(*refs):
    count = len(refs) // 2
    sems = refs[-1]
    copies = [pltpu.make_async_copy(refs[i], refs[count + i], sems.at[i]) for i in range(count)]
    for copy in copies:
        copy.start()
    for copy in copies:
        copy.wait()


def on_device(n_dp, n_e, tokens, cotangent, router, in_weights, out_weights):
    _, patches, width = tokens.shape
    ff = in_weights.shape[2]
    slots = router.shape[1]
    n_x = n_dp // QUAD
    share = ff // n_dp
    tile_rows = min(8, slots)
    n_tiles = slots // tile_rows * (width // LANES)
    vmem = pltpu.VMEM
    dma = pltpu.SemaphoreType.DMA
    shapes = (
        ((patches, width), LOW),
        ((slots, width), F32),
        ((share, width), LOW),
        ((share, width), LOW),
    )
    results = pl.pallas_call(
        functools.partial(kernel, n_dp, n_e),
        out_shape=[vmem(*shape) for shape in shapes],
        in_specs=[pl.BlockSpec(memory_space=pl.ANY)] * 5,
        out_specs=[pl.BlockSpec(memory_space=vmem)] * 4,
        scratch_shapes=[
            vmem((patches, width), LOW),
            vmem((patches, width), LOW),
            vmem((slots, width), LOW),
            vmem((width, ff), LOW),
            vmem((ff, width), LOW),
            vmem((slots * ROWS, LANES), F32),
            vmem((slots * ROWS, LANES), F32),
            *[vmem((slots, ROWS, LANES), LOW)] * 4,
            vmem((n_x, 2, slots, width), LOW),
            vmem((n_x, slots, 2 * ff // n_x), LOW),
            vmem((n_x, slots, 2 * ff // n_x), LOW),
            vmem((2, QUAD, share, width), F32),
            vmem((n_tiles, tile_rows, LANES), F32),
            vmem((n_dp, tile_rows, LANES), F32),
            vmem((n_e, tile_rows, LANES), F32),
            vmem((n_tiles, tile_rows, LANES), F32),
            vmem((2, 2, share, width), LOW),
            vmem((2, 2, share, width), LOW),
            vmem((2, share, width), LOW),
            vmem((2, share, width), LOW),
            dma((5,)),
            dma((14,)),
            dma((14,)),
            dma((n_x // 2, 2)),
            dma((n_x // 2, 2)),
        ],
        compiler_params=pltpu.CompilerParams(
            collective_id=0, has_side_effects=True, vmem_limit_bytes=56 * 2**20
        ),
        cost_estimate=pl.CostEstimate(flops=10**9, bytes_accessed=10**7, transcendentals=10**5),
    )(tokens[0], cotangent[0], router.T, in_weights[0], out_weights[0])
    token_grad, router_grad, in_grad, out_grad = pl.pallas_call(
        deliver,
        out_shape=[jax.ShapeDtypeStruct(*shape) for shape in shapes],
        in_specs=[pl.BlockSpec(memory_space=vmem)] * 4,
        out_specs=[pl.BlockSpec(memory_space=pl.ANY)] * 4,
        scratch_shapes=[dma((4,))],
    )(*[pltpu.with_memory_space_constraint(result, vmem) for result in results])
    return token_grad[None], router_grad.T, in_grad[:, None], out_grad[:, None]


def solution(mesh):
    image = P(("dp", "expert"), None, None)
    expert = P("expert", None, None)
    grad = P("dp", "expert", None)
    return jax.shard_map(
        functools.partial(on_device, mesh.shape["dp"], mesh.shape["expert"]),
        mesh=mesh,
        in_specs=(image, image, P(), expert, expert),
        out_specs=(image, P(), grad, grad),
        check_vma=False,
    )
```

```python
import functools

import jax
import jax.numpy as jnp
from jax import lax
from jax.experimental import pallas as pl
from jax.experimental.pallas import tpu as pltpu
from jax.sharding import PartitionSpec as P

MESH = pl.DeviceIdType.MESH
LOW = jnp.bfloat16
F32 = jnp.float32
QUAD = 4
LANES = 128
ROWS = 16
half_root = 0.7071067811865476
inv_root_two_pi = 0.3989422804014327


def dot(a, b, dims):
    return lax.dot_general(a, b, (dims, ((), ())), preferred_element_type=F32)


NN = ((1,), (0,))
NT = ((1,), (1,))
TN = ((0,), (0,))


def pack(stage, dst, first, second):
    slots, width = first.shape
    parts = width // LANES
    for i, value in enumerate((first, second)):
        for j in range(parts):
            stage[pl.ds(i * parts + j, slots, stride=ROWS), :] = value[:, j * LANES : (j + 1) * LANES]
    dst[...] = stage[...].reshape(slots, ROWS, LANES).astype(LOW)


def unpack(stage, src, width):
    slots = src.shape[0]
    parts = width // LANES
    stage[...] = src[...].astype(F32).reshape(slots * ROWS, LANES)
    both = []
    for i in range(2):
        columns = [stage[pl.ds(i * parts + j, slots, stride=ROWS), :] for j in range(parts)]
        both.append(jnp.concatenate(columns, axis=1).astype(LOW))
    return both


def kernel(
    n_dp, n_e,
    tok_h, cot_h, rt_h, w1_h, w2_h,
    tg, rg, g1, g2,
    tok, cot, rt, w1, w2, stage, stage_b,
    s1, r1, s2, r2, rows, msgs, part, total,
    tiles, tiles_in, sum_e, tiles_out,
    core_out, core_in, pair_out, pair_in,
    load, send, recv, ring_send, ring_recv,
):
    dp, e = lax.axis_index("dp"), lax.axis_index("expert")
    n_x = n_dp // QUAD
    x, q = dp // QUAD, lax.rem(dp, QUAD)
    slots = n_e
    width = tok.shape[1]
    ff = w1.shape[1]
    share = ff // n_dp
    n_tiles = tiles.shape[0]
    tile_rows = tiles.shape[1]
    across = width // LANES

    def each(count, body):
        far = max(1, count * 3 // 8)
        for o in (*range(far, count), *range(1, far)):
            body(o)

    def to_experts(body):
        each(n_e, lambda o: body(lax.rem(e + o, n_e)))

    def to_replicas(body):
        each(n_dp, lambda o: body(lax.rem(dp + o, n_dp)))

    barrier = pltpu.get_barrier_semaphore()

    def greet(device):
        pl.semaphore_signal(barrier, inc=1, device_id=device, device_id_type=MESH)

    to_experts(lambda peer: greet((dp, peer)))
    to_replicas(lambda peer: greet((peer, e)))

    loads = [
        pltpu.make_async_copy(src, dst, load.at[i])
        for i, (src, dst) in enumerate(((rt_h, rt), (tok_h, tok), (cot_h, cot), (w1_h, w1), (w2_h, w2)))
    ]
    for copy in loads:
        copy.start()
    stage[...] = jnp.zeros_like(stage)

    def remote(src, dst, at, device):
        return pltpu.make_async_remote_copy(
            src_ref=src, dst_ref=dst, send_sem=send.at[at], recv_sem=recv.at[at],
            device_id=device, device_id_type=MESH,
        )

    next_e = (dp, lax.rem(e + 1, n_e))
    next_x = (lax.rem(x + 1, n_x) * QUAD + q, e)
    next_dp = (lax.rem(dp + 1, n_dp), e)

    half = n_x // 2
    right = next_x
    left = (lax.rem(x + n_x - 1, n_x) * QUAD + q, e)

    def ring(s, sender):
        a = lax.rem(x - (s - 1 + sender) + n_x, n_x)
        b = lax.rem(x + s - 1 + sender, n_x)
        blocks = (rows.at[a], rows.at[b]) if s < half else (rows.at[a, 0], rows.at[b, 1])
        return [
            pltpu.make_async_remote_copy(
                src_ref=block, dst_ref=block, send_sem=ring_send.at[s - 1, i], recv_sem=ring_recv.at[s - 1, i],
                device_id=device, device_id_type=MESH,
            )
            for i, (block, device) in enumerate(zip(blocks, (right, left)))
        ]

    def ring_start(s):
        for copy in ring(s, 0):
            copy.start()

    def ring_arrived(s):
        for copy in ring(s, 1):
            copy.wait_recv()

    def all_of(ref, count, at, device):
        return remote(ref.at[pl.ds(0, count)], ref.at[pl.ds(0, count)], at, device)

    loads[0].wait()
    loads[1].wait()
    logits = dot(rt[...], tok[...], NT)
    over_patches = jnp.exp(logits - jnp.max(logits, axis=1, keepdims=True))
    dispatch = over_patches / jnp.sum(over_patches, axis=1, keepdims=True)
    over_slots = jnp.exp(logits - jnp.max(logits, axis=0, keepdims=True))
    combine = over_slots / jnp.sum(over_slots, axis=0, keepdims=True)
    dispatch_low = dispatch.astype(LOW)
    combine_low = combine.astype(LOW)
    slot_inputs = dot(dispatch_low, tok[...], NN)
    loads[2].wait()
    slot_cotan = dot(combine_low, cot[...], NN)
    pack(stage, s1, slot_inputs, slot_cotan)
    pl.semaphore_wait(barrier, n_e - 1 + n_dp - 1)

    @to_experts
    def _(peer):
        remote(s1.at[peer], r1.at[e], 0, (dp, peer)).start()

    r1[e] = s1[e]
    all_of(r1, n_e - 1, 0, next_e).wait_recv()

    rows_in, rows_cotan = unpack(stage_b, r1, width)
    rows[x, 0] = rows_in
    rows[x, 1] = rows_cotan

    ring_start(1)

    loads[3].wait()
    loads[4].wait()
    block = ff // n_x
    pair = 2 * block
    per = 2 if ff % (2 * pair) == 0 else 1
    step = per * pair
    outputs = jnp.zeros((slots, width), F32)
    grads = jnp.zeros((slots, width), F32)
    is_first = lax.broadcasted_iota(jnp.int32, (slots, pair), 1) < block
    for k in range(ff // step):
        first = w1[:, k * step : (k + 1) * step]
        second = w2[k * step : (k + 1) * step, :]
        pre_act = dot(rows_in, first, NN)
        hidden_grad = dot(rows_cotan, second, NT)
        normal_cdf = 0.5 * (1.0 + lax.erf(pre_act * half_root))
        normal_pdf = jnp.exp(-0.5 * pre_act * pre_act) * inv_root_two_pi
        hidden = pre_act * normal_cdf
        pre_grad = hidden_grad * (normal_cdf + pre_act * normal_pdf)
        outputs += dot(hidden.astype(LOW), second, NN)
        grads += dot(pre_grad.astype(LOW), first, NT)
        for i in range(per):
            p_part = pre_grad[:, i * pair : (i + 1) * pair]
            h_part = hidden[:, i * pair : (i + 1) * pair]
            at = 2 * (k * per + i)
            msgs[at] = jnp.where(is_first, p_part, pltpu.roll(h_part, block, 1)).astype(LOW)
            msgs[at + 1] = jnp.where(is_first, pltpu.roll(p_part, block, 1), h_part).astype(LOW)
            for to in (at, at + 1):

                @pl.when(x != to)
                def _():
                    remote(msgs.at[to], part.at[x], 3, (to * QUAD + q, e)).start()
    pack(stage, s2, outputs, grads)

    @to_experts
    def _(peer):
        remote(s2.at[peer], r2.at[e], 2, (dp, peer)).start()

    part[x] = msgs[x]
    r2[e] = s2[e]
    for s in range(1, half - 2):
        ring_arrived(s)
        ring_start(s + 1)
    all_of(r2, n_e - 1, 2, next_e).wait_recv()

    slot_outputs, input_grads = unpack(stage_b, r2, width)
    combine_grad = dot(slot_outputs, cot[...], NT)
    dispatch_grad = dot(input_grads, tok[...], NT)
    logit_grad = combine * (combine_grad - jnp.sum(combine * combine_grad, axis=0, keepdims=True))
    logit_grad += dispatch * (dispatch_grad - jnp.sum(dispatch * dispatch_grad, axis=1, keepdims=True))
    logit_low = logit_grad.astype(LOW)
    router_part = dot(logit_low, tok[...], NN)
    for t in range(n_tiles):
        i, j = divmod(t, across)
        tiles[t] = router_part[i * tile_rows : (i + 1) * tile_rows, j * LANES : (j + 1) * LANES]

    @to_replicas
    def _(peer):
        @pl.when(peer < n_tiles)
        def _():
            remote(tiles.at[peer], tiles_in.at[dp], 4, (peer, e)).start()

    for s in range(max(1, half - 2), half - 1):
        ring_arrived(s)
        ring_start(s + 1)
    weights = jnp.concatenate([dispatch_low, logit_low], axis=0)
    values = jnp.concatenate([input_grads, rt[...]], axis=0)
    tg[...] = dot(weights, values, TN).astype(LOW)

    if half > 1:
        ring_arrived(half - 1)
        ring_start(half)

    @pl.when(dp < n_tiles)
    def _():
        tiles_in[dp] = tiles[dp]
        all_of(tiles_in, n_dp - 1, 4, next_dp).wait_recv()
        sum_e[e] = jnp.sum(tiles_in[...], axis=0)

        @to_experts
        def _(peer):
            remote(sum_e.at[e], sum_e.at[e], 5, (dp, peer)).start()

    ring_arrived(half)
    all_of(part, n_x - 1, 3, next_x).wait_recv()
    wide = part[...].reshape(n_x * slots, pair).T
    z, core = q // 2, lax.rem(q, 2)
    other_core = (x * QUAD + z * 2 + 1 - core, e)
    other_pair = (x * QUAD + (1 - z) * 2 + core, e)
    blocks = ((1 - z) * 2, z * 2)
    core_copies = [[remote(core_out.at[k, i], core_in.at[k, i], 8 + 2 * k + i, other_core) for i in range(2)] for k in range(2)]
    pair_copies = [remote(pair_out.at[i], pair_in.at[i], 12 + i, other_pair) for i in range(2)]
    for i in range(2):
        values = rows[:, i].reshape(n_x * slots, width)
        total[i] = dot(wide[i * block : (i + 1) * block], values, NN).reshape(QUAD, share, width)
        core_out[0, i] = total[i, blocks[0] + 1 - core].astype(LOW)
        core_copies[0][i].start()
    for i in range(2):
        core_out[1, i] = total[i, blocks[1] + 1 - core].astype(LOW)
        core_copies[1][i].start()

    for i in range(2):
        core_copies[0][i].wait_recv()
        pair_out[i] = (total[i, blocks[0] + core] + core_in[0, i].astype(F32)).astype(LOW)
        pair_copies[i].start()

    @pl.when(dp < n_tiles)
    def _():
        all_of(sum_e, n_e - 1, 5, next_e).wait_recv()
        tiles_out[dp] = jnp.sum(sum_e[...], axis=0)

        @to_replicas
        def _(peer):
            remote(tiles_out.at[dp], tiles_out.at[dp], 6, (peer, e)).start()

    for i, out in enumerate((g1, g2)):
        core_copies[1][i].wait_recv()
        pair_copies[i].wait_recv()
        out[...] = (total[i, q] + core_in[1, i].astype(F32) + pair_in[i].astype(F32)).astype(LOW)

    @pl.when(dp < n_tiles)
    def _():
        all_of(tiles_out, n_tiles - 1, 6, next_dp).wait_recv()

    @pl.when(dp >= n_tiles)
    def _():
        all_of(tiles_out, n_tiles, 6, next_dp).wait_recv()

    for t in range(n_tiles):
        i, j = divmod(t, across)
        rg[i * tile_rows : (i + 1) * tile_rows, j * LANES : (j + 1) * LANES] = tiles_out[t]

    all_of(s1, n_e - 1, 0, next_e).wait_send()
    for s in range(1, half + 1):
        for copy in ring(s, 0):
            copy.wait_send()
    all_of(s2, n_e - 1, 2, next_e).wait_send()
    all_of(msgs, n_x - 1, 3, next_x).wait_send()
    for copy in core_copies[0] + core_copies[1] + pair_copies:
        copy.wait_send()

    @pl.when(dp < n_tiles)
    def _():
        all_of(tiles, n_tiles - 1, 4, next_dp).wait_send()
        all_of(sum_e, n_e - 1, 5, next_e).wait_send()
        all_of(tiles_in, n_dp - 1, 6, next_dp).wait_send()

    @pl.when(dp >= n_tiles)
    def _():
        all_of(tiles, n_tiles, 4, next_dp).wait_send()


def deliver(*refs):
    count = len(refs) // 2
    sems = refs[-1]
    copies = [pltpu.make_async_copy(refs[i], refs[count + i], sems.at[i]) for i in range(count)]
    for copy in copies:
        copy.start()
    for copy in copies:
        copy.wait()


def on_device(n_dp, n_e, tokens, cotangent, router, in_weights, out_weights):
    _, patches, width = tokens.shape
    ff = in_weights.shape[2]
    slots = router.shape[1]
    n_x = n_dp // QUAD
    share = ff // n_dp
    tile_rows = min(8, slots)
    n_tiles = slots // tile_rows * (width // LANES)
    vmem = pltpu.VMEM
    dma = pltpu.SemaphoreType.DMA
    shapes = (
        ((patches, width), LOW),
        ((slots, width), F32),
        ((share, width), LOW),
        ((share, width), LOW),
    )
    results = pl.pallas_call(
        functools.partial(kernel, n_dp, n_e),
        out_shape=[vmem(*shape) for shape in shapes],
        in_specs=[pl.BlockSpec(memory_space=pl.ANY)] * 5,
        out_specs=[pl.BlockSpec(memory_space=vmem)] * 4,
        scratch_shapes=[
            vmem((patches, width), LOW),
            vmem((patches, width), LOW),
            vmem((slots, width), LOW),
            vmem((width, ff), LOW),
            vmem((ff, width), LOW),
            vmem((slots * ROWS, LANES), F32),
            vmem((slots * ROWS, LANES), F32),
            *[vmem((slots, ROWS, LANES), LOW)] * 4,
            vmem((n_x, 2, slots, width), LOW),
            vmem((n_x, slots, 2 * ff // n_x), LOW),
            vmem((n_x, slots, 2 * ff // n_x), LOW),
            vmem((2, QUAD, share, width), F32),
            vmem((n_tiles, tile_rows, LANES), F32),
            vmem((n_dp, tile_rows, LANES), F32),
            vmem((n_e, tile_rows, LANES), F32),
            vmem((n_tiles, tile_rows, LANES), F32),
            vmem((2, 2, share, width), LOW),
            vmem((2, 2, share, width), LOW),
            vmem((2, share, width), LOW),
            vmem((2, share, width), LOW),
            dma((5,)),
            dma((14,)),
            dma((14,)),
            dma((n_x // 2, 2)),
            dma((n_x // 2, 2)),
        ],
        compiler_params=pltpu.CompilerParams(
            collective_id=0, has_side_effects=True, vmem_limit_bytes=56 * 2**20
        ),
        cost_estimate=pl.CostEstimate(flops=10**9, bytes_accessed=10**7, transcendentals=10**5),
    )(tokens[0], cotangent[0], router.T, in_weights[0], out_weights[0])
    token_grad, router_grad, in_grad, out_grad = pl.pallas_call(
        deliver,
        out_shape=[jax.ShapeDtypeStruct(*shape) for shape in shapes],
        in_specs=[pl.BlockSpec(memory_space=vmem)] * 4,
        out_specs=[pl.BlockSpec(memory_space=pl.ANY)] * 4,
        scratch_shapes=[dma((4,))],
    )(*[pltpu.with_memory_space_constraint(result, vmem) for result in results])
    return token_grad[None], router_grad.T, in_grad[:, None], out_grad[:, None]


def solution(mesh):
    image = P(("dp", "expert"), None, None)
    expert = P("expert", None, None)
    grad = P("dp", "expert", None)
    return jax.shard_map(
        functools.partial(on_device, mesh.shape["dp"], mesh.shape["expert"]),
        mesh=mesh,
        in_specs=(image, image, P(), expert, expert),
        out_specs=(image, P(), grad, grad),
        check_vma=False,
    )
```
